128 devices in a mesh: intra: 16 (over z, x), cross: 8 (over y, core).
Axes of the slice: x: 4, y: 4, z: 4, core: 2. Of those that a mesh axis runs over, the one named last changes fastest.
Arguments:
- tokens: bfloat16 [131072, 4096], P(('intra', 'cross')), may hold values from -80 to 80
- norm_gain: bfloat16 [4096], P(('intra', 'cross')), may hold values from 0.5 to 1.5
- weight_codes: bfloat16 [4096, 1024], P(('intra', 'cross')), may hold values from -127 to 127, as said below
- block_scales: bfloat16 [2048], P(('intra', 'cross')), may hold values from 9.9658966e-05 to 0.00039863586
- upstream: bfloat16 [131072, 1024], P(('intra', 'cross')), may hold values from -6 to 6
- loss_mask: int32 [131072], P(('intra', 'cross')), may hold values 0 or 1
Outputs:
- projected: bfloat16 [131072, 1024], P(('intra', 'cross'))
- grad_tokens: bfloat16 [131072, 4096], P(('intra', 'cross'))
- grad_weight: float32 [4096, 1024], P(('intra', 'cross'))
- grad_gain: float32 [4096], P(('intra', 'cross'))
The draws below stay inside these ranges and needn't reach their ends.
Inputs may be any that keep to these rules, and one draw needn't show every extreme that they name: `weight_codes`: integer values.
All inputs are finite; a program needn't handle non-finite values. No bound on the sum of `loss_mask` on one device may be relied on, other than what follows from the above.
Results may differ from the reference program's by a relative error of at most 0.0058.
Values may be sent and summed in bfloat16 or wider, within the bound.
A program may use at most 192 MiB of HBM per device.

```python
import math
import jax
import jax.numpy as jnp
from jax import lax

D = 4096
TOK_DEV = 1024
KV = 1024
ROWS_BLK = 2
TOKENS = 131072
N_INTRA = 16
N_CROSS = 8


def draw_tokens(key, part):
    key = jax.random.fold_in(key, 11)
    first, second, third = jax.random.split(key, 3)
    row_scale = jnp.exp(jax.random.uniform(second, (TOKENS, 1), jnp.float32, 0.0, math.log(10.0)))
    col_scale = jnp.exp(jax.random.uniform(third, (1, D), jnp.float32, math.log(0.5), math.log(2.0)))
    base = jax.random.truncated_normal(first, -4.0, 4.0, (TOKENS, D), jnp.float32)
    return (base * row_scale * col_scale).astype(jnp.bfloat16)


def draw_weight_codes(key, part):
    key = jax.random.fold_in(key, 23)
    values = jax.random.randint(key, (D, KV), -127, 128, jnp.int32)
    return values.astype(jnp.float32).astype(jnp.bfloat16)


def touch_ends(entries, own_key, least, high):
    dims = entries.shape
    place = [jax.random.randint(jax.random.fold_in(own_key, axis), (), 0, dims[axis]) for axis in range(len(dims))]
    entries = entries.at[tuple(place)].set(least)
    longest = dims.index(max(dims))
    place[longest] = (place[longest] + 1) % dims[longest]
    return entries.at[tuple(place)].set(high)


def steps_of(key, extent, cuts, smallest, top_value):
    loudness = 1.0
    for axis_at, blocks in cuts:
        steps = jax.random.uniform(jax.random.fold_in(jax.random.fold_in(key, 6), axis_at), (blocks,), jnp.float32, smallest / len(cuts), top_value / len(cuts))
        loudness = loudness * jnp.repeat(jnp.exp(steps), extent[axis_at] // blocks).reshape((-1,) + (1,) * (len(extent) - 1 - axis_at))
    return loudness


def normal_values(own_key, dims, deviation, limit, shards=(), dtype=jnp.bfloat16):
    array = deviation * jax.random.normal(own_key, dims, jnp.float32)
    if shards:
        array = array * steps_of(own_key, dims, shards, -0.22, 0.18)
    return jnp.clip(array, -limit, limit).astype(dtype)


def setup_inputs(seed: int = 0) -> dict:
    streams_of = jax.random.split(jax.random.key(seed), 7)
    tokens = draw_tokens(jax.random.fold_in(streams_of[6], 71), 0)
    norm_gain = jnp.clip(1.0 + 0.1 * jax.random.normal(streams_of[1], (D,), jnp.float32), 0.5, 1.5).astype(jnp.bfloat16)
    weight_codes = draw_weight_codes(jax.random.fold_in(streams_of[6], 71), 0)
    block_scales = jnp.clip(jnp.exp(math.log(0.00039863586) - 1.3862944 * jax.random.uniform(streams_of[3], (D // ROWS_BLK,), jnp.float32) ** steps_of(streams_of[3], (D // ROWS_BLK,), ((0, 128),), -0.2, 0.2)), 9.965896606445312e-05, 0.00039863586).astype(jnp.bfloat16)
    upstream = normal_values(streams_of[4], (TOKENS, KV), 1.0, 6.0, ((0, 128),))
    loss_mask = touch_ends((jax.random.randint(streams_of[5], (TOKENS,), 0, 4) < 3).astype(jnp.int32), jax.random.fold_in(streams_of[5], 1), 0, 1)
    return {"tokens": tokens, "norm_gain": norm_gain, "weight_codes": weight_codes, "block_scales": block_scales, "upstream": upstream, "loss_mask": loss_mask}


def dequantize(weight_codes, block_scales):
    row_scales = jnp.repeat(block_scales.astype(jnp.float32), ROWS_BLK)
    return (weight_codes.astype(jnp.float32) * row_scales[:, None]).astype(jnp.bfloat16)

def reference(tokens, norm_gain, weight_codes, block_scales, upstream, loss_mask):
    weight = dequantize(weight_codes, block_scales)
    gains = norm_gain.astype(jnp.float32)
    blocks = N_INTRA * N_CROSS
    token_blocks = tokens.reshape(blocks, TOK_DEV, D)
    grad_blocks = upstream.reshape(blocks, TOK_DEV, KV)
    mask_blocks = loss_mask.reshape(blocks, TOK_DEV)

    def one_block(carry, inputs):
        block_tokens, block_up, block_mask = inputs
        values = block_tokens.astype(jnp.float32)
        inverse = lax.rsqrt(lax.optimization_barrier(jnp.mean(values * values, axis=1, keepdims=True)) + 1e-05)
        unit_rows = values * inverse
        normed = (unit_rows * gains[None, :]).astype(jnp.bfloat16)
        projected = jnp.dot(normed, weight, preferred_element_type=jnp.float32).astype(jnp.bfloat16)
        masked = block_up * block_mask.astype(jnp.bfloat16)[:, None]
        grad_normed = jnp.dot(masked, weight.T, preferred_element_type=jnp.float32)
        grad_scaled = grad_normed * gains[None, :]
        grad_tokens = (inverse * (grad_scaled - unit_rows * lax.optimization_barrier(jnp.mean(grad_scaled * unit_rows, axis=1, keepdims=True)))).astype(jnp.bfloat16)
        part_weight = jnp.dot(normed.T, masked, preferred_element_type=jnp.float32)
        part_gain = lax.optimization_barrier(jnp.sum(grad_normed * unit_rows, axis=0))
        return ((carry[0] + part_weight, carry[1] + part_gain), (projected, grad_tokens))
    start = (jnp.zeros((D, KV), jnp.float32), jnp.zeros((D,), jnp.float32))
    sums, outputs = lax.scan(one_block, start, (token_blocks, grad_blocks, mask_blocks))
    projected = outputs[0].reshape(TOKENS, KV)
    grad_tokens = outputs[1].reshape(TOKENS, D)
    return (projected, grad_tokens, sums[0], sums[1])
```

```python
import jax
import jax.numpy as jnp
from jax import lax
from jax.experimental import pallas as pl
from jax.experimental.pallas import tpu as pltpu
from jax.sharding import PartitionSpec as P

MESH = pl.DeviceIdType.MESH
F32 = jnp.float32
BF16 = jnp.bfloat16
D = 4096
KV = 1024
TOK = 1024
ROWS = 32
TILE = 256
COLS = (384, 384, 256)
ORDERS = ((0, 1, 2), (1, 2, 0), (2, 0, 1))
PARTS = range(3)
STEPS = (1, -1, 2)
CHUNKS = (0, 1, -1, 2)
PLANES = (0, -1, 1, 2)


def piece(part, stage, pos, at, half=None):
    order = ORDERS[part]
    index = [None, None, None, pos[3], slice(None), slice(None)]
    for axis in order[:stage]:
        index[axis] = pos[axis]
    index[order[stage]] = at
    free = order[stage + 1 :]
    for axis in free:
        index[axis] = slice(None)
    if half is not None:
        if free:
            index[min(free)] = slice(2 * half, 2 * half + 2)
        else:
            index[4] = slice(16 * half, 16 * half + 16)
    return tuple(index)


def kernel(
    tokens, upstream, mask, codes, scales, gain,
    proj, tok, grad_weight, grad_gain,
    up, masked, mi, inv, coef, acc, mine,
    w0, w1, w2, g0, g1, g2, c0, c1, c2,
    r00, r10, r20, r01, r11, r21, r02, r12, r22,
    load_sem, ag_send, ag_recv, fwd_send, fwd_recv, pair_send, pair_recv, rs_send, rs_recv,
):
    gathered = (w0, w1, w2)
    sums = (g0, g1, g2)
    pair = (c0, c1, c2)
    landing = ((r00, r01, r02), (r10, r11, r12), (r20, r21, r22))
    intra, cross = lax.axis_index("intra"), lax.axis_index("cross")
    z, x, y, core = intra // 4, intra % 4, cross // 2, cross % 2
    pos = (z, x, y, core)

    def device(at):
        return (at[0] * 4 + at[1], at[2] * 2 + at[3])

    def shifted(axis, step):
        return (pos[axis] + step + 4) % 4

    def beside(axis, step):
        return device(pos[:axis] + (shifted(axis, step),) + pos[axis + 1 :])

    sibling = device((z, x, y, 1 - core))
    blocks = [shifted(0, step) for step in (2, 1, 3, 0)]

    def remote(src, dst, send, recv, to):
        return pltpu.make_async_remote_copy(
            src_ref=src, dst_ref=dst, send_sem=send, recv_sem=recv, device_id=to, device_id_type=MESH
        )

    def ag_copy(part, stage, slot, arriving):
        axis = ORDERS[part][2 - stage]
        at = shifted(axis, -STEPS[slot]) if arriving else pos[axis]
        ref = gathered[part].at[piece(part, 2 - stage, pos, at)]
        number = part * 22 + stage * 3 + slot
        return remote(ref, ref, ag_send.at[number], ag_recv.at[number], beside(axis, STEPS[slot]))

    def ag_chunk(part, chunk, slot, arriving):
        far, near, last = ORDERS[part]
        side = (1, -1, 1, -1)[slot]
        hops = 1 if slot < 2 else 2
        came = hops if arriving else hops - 1
        index = [None, None, None, core, slice(None), slice(None)]
        index[far] = shifted(far, -side * came)
        index[near] = shifted(near, -CHUNKS[chunk])
        index[last] = slice(None) if slot < 2 else slice(2 * (slot - 2), 2 * (slot - 2) + 2)
        ref = gathered[part].at[tuple(index)]
        number = part * 22 + 6 + chunk * 4 + slot
        return remote(ref, ref, ag_send.at[number], ag_recv.at[number], beside(far, side))

    def forward(part, chunk, slot, arriving):
        far, near, _ = ORDERS[part]
        index = [slice(None), slice(None), slice(None), (1 - core) if arriving else core, slice(None), slice(None)]
        index[far] = shifted(far, PLANES[slot])
        if slot:
            index[near] = shifted(near, -CHUNKS[chunk])
        ref = gathered[part].at[tuple(index)]
        number = part * 13 + (slot and 3 * chunk + slot)
        return remote(ref, ref, fwd_send.at[number], fwd_recv.at[number], sibling)

    def ag_send_out(stage):
        for part in PARTS:
            for slot in range(3):
                ag_copy(part, stage, slot, False).start()

    def ag_wait(stage, slots=range(3)):
        for part in PARTS:
            for slot in slots:
                ag_copy(part, stage, slot, True).wait_recv()

    def chunk_out(chunk):
        for part in PARTS:
            ag_chunk(part, chunk, 0, False).start()
            ag_chunk(part, chunk, 1, False).start()

    def chunk_pass(chunk):
        for part in PARTS:
            for side in (0, 1):
                ag_chunk(part, chunk, side, True).wait_recv()
                ag_chunk(part, chunk, 2 + side, False).start()
                forward(part, chunk, 1 + side, False).start()

    def chunk_end(chunk):
        for part in PARTS:
            ag_chunk(part, chunk, 2, True).wait_recv()
            ag_chunk(part, chunk, 3, True).wait_recv()
            forward(part, chunk, 3, False).start()

    def forward_wait(slot):
        for part in PARTS:
            for chunk in range(4 if slot else 1):
                forward(part, chunk, slot, True).wait_recv()

    def pair_copy(part, i):
        at, k = blocks[i], part * 4 + i
        index = (at, slice(None), slice(None), 1 - core)
        return remote(sums[part].at[index], pair[part].at[at], pair_send.at[k], pair_recv.at[k], sibling)

    def pair_out(i):
        for part in PARTS:
            pair_copy(part, i).start()

    def pair_add(i):
        at = blocks[i]
        for part in PARTS:
            pair_copy(part, i).wait_recv()

            def add(xi, carry, part=part):
                own = sums[part][at, xi, :, core].astype(F32)
                sums[part][at, xi, :, core] = (own + pair[part][at, xi].astype(F32)).astype(BF16)
                return carry

            lax.fori_loop(0, 4, add, 0)

    def rs_remote(part, stage, slot, index, axis, step):
        number = part * 18 + (0, 12, 15)[stage] + slot
        return remote(
            sums[part].at[index], landing[part][stage].at[slot],
            rs_send.at[number], rs_recv.at[number], beside(axis, step),
        )

    def z_copy(slot):
        step, half, side = ((2, 0, 1), (2, 1, -1), (1, 0, 1), (1, 1, 1), (-1, 0, -1), (-1, 1, -1))[slot]
        return rs_remote(0, 0, slot, piece(0, 0, pos, shifted(0, step), half), 0, side)

    def block_index(part, i, at):
        index = [blocks[i], slice(None), slice(None), core, slice(None), slice(None)]
        index[ORDERS[part][0]] = at
        return tuple(index)

    def block_copy(part, i, kind):
        axis = ORDERS[part][0]
        side = ((1 if i < 2 else -1), 1, -1)[kind]
        step = (2, 1, -1)[kind]
        return rs_remote(part, 0, kind * 4 + i, block_index(part, i, shifted(axis, step)), axis, side)

    def rs_begin(i):
        for slot in ((0, 1), (3,), (4,), ())[i]:
            z_copy(slot).start()
        for part in (1, 2):
            block_copy(part, i, 0).start()
            block_copy(part, i, 2 if i < 2 else 1).start()

    def rs_pass_z(slot):
        out = (2, 5)[slot]
        z_copy(slot).wait_recv()
        index = piece(0, 0, pos, shifted(0, (1, -1)[slot]), slot)
        sums[0][index] = (sums[0][index].astype(F32) + landing[0][0][slot].astype(F32)).astype(BF16)
        z_copy(out).start()

    def rs_pass(i):
        for part in (1, 2):
            block_copy(part, i, 0).wait_recv()
            step, kind = (1, 1) if i < 2 else (-1, 2)
            index = block_index(part, i, shifted(ORDERS[part][0], step))
            sums[part][index] = (sums[part][index].astype(F32) + landing[part][0][i].astype(F32)).astype(BF16)
            block_copy(part, i, kind).start()

    def rs_own_z():
        for slot in (2, 3, 4, 5):
            z_copy(slot).wait_recv()
        for half in (0, 1):
            index = piece(0, 0, pos, z, half)
            sums[0][index] = (
                sums[0][index].astype(F32)
                + landing[0][0][2 + half].astype(F32)
                + landing[0][0][4 + half].astype(F32)
            ).astype(BF16)

    def rs_own(part):
        for i in range(4):
            block_copy(part, i, 1).wait_recv()
            block_copy(part, i, 2).wait_recv()
            index = block_index(part, i, pos[ORDERS[part][0]])
            sums[part][index] = (
                sums[part][index].astype(F32)
                + landing[part][0][4 + i].astype(F32)
                + landing[part][0][8 + i].astype(F32)
            ).astype(BF16)

    def rs_copy(part, stage, slot):
        axis = ORDERS[part][stage]
        index = piece(part, stage, pos, shifted(axis, STEPS[slot]))
        return rs_remote(part, stage, slot, index, axis, STEPS[slot])

    def rs_send_out(part, stage):
        for slot in (2, 0, 1):
            rs_copy(part, stage, slot).start()

    def rs_total(part, stage):
        index = piece(part, stage, pos, pos[ORDERS[part][stage]])
        total = sums[part][index].astype(F32)
        for slot in range(3):
            rs_copy(part, stage, slot).wait_recv()
            total = total + landing[part][stage][slot].astype(F32)
        if stage == 1:
            sums[part][index] = total.astype(BF16)
        return total

    def load(i):
        rows = pl.ds(i * TILE, TILE)
        return (
            pltpu.make_async_copy(tokens.at[rows], tok.at[rows], load_sem.at[i]),
            pltpu.make_async_copy(upstream.at[rows], up.at[rows], load_sem.at[4 + i]),
        )

    def norms(i):
        for copy in load(i):
            copy.wait()

        def some(j, carry):
            rows = pl.ds(pl.multiple_of(i * TILE + j * 64, 64), 64)
            values = tok[rows, :].astype(F32)
            inverse = lax.rsqrt(jnp.sum(values * values, axis=1, keepdims=True) * (1.0 / D) + 1e-05)
            inv[rows, :] = inverse
            kept = up[rows, :].astype(F32) * coef[rows, :]
            masked[rows, :] = kept.astype(BF16)
            mi[rows, :] = (kept * inverse).astype(BF16)
            return carry

        lax.fori_loop(0, TILE // 64, some, 0)

    def partial_sums(i):
        zi = blocks[i]
        columns = pl.ds(pl.multiple_of(zi * 1024, 1024), 1024)
        part_sum = lax.dot_general(
            tok[:, columns], mi[...], (((0,), (0,)), ((), ())), preferred_element_type=F32
        ).astype(BF16)
        start = 0
        for part in PARTS:
            cols = part_sum[:, start : start + COLS[part]]
            sums[part][zi] = cols.reshape(4, 4, 2, ROWS, COLS[part])
            start += COLS[part]

    def weight_block(zi):
        return jnp.concatenate(
            [gathered[part][zi].reshape(1024, COLS[part]) for part in PARTS], axis=1
        )

    def project(zi):
        columns = pl.ds(zi * 1024, 1024)
        value = jnp.dot(tok[:, columns], weight_block(zi), preferred_element_type=F32)
        if zi == 0:
            acc[...] = value
        else:
            acc[...] += value

    def project_end():
        def some(j, carry):
            rows = pl.ds(pl.multiple_of(j * 64, 64), 64)
            inverse = inv[rows, :]
            value = acc[rows, :] * inverse
            proj[rows, :] = value.astype(BF16)
            mean = jnp.sum(value * masked[rows, :].astype(F32), axis=1, keepdims=True) * (1.0 / D)
            coef[rows, :] = mean * inverse
            return carry

        lax.fori_loop(0, TOK // 64, some, 0)

    def backward(zi):
        columns = pl.ds(zi * 1024, 1024)
        value = lax.dot_general(
            masked[...], weight_block(zi), (((1,), (1,)), ((), ())), preferred_element_type=F32
        )
        value = inv[...] * (value - tok[:, columns].astype(F32) * coef[...])
        tok[:, columns] = value.astype(BF16)

    for i in range(4):
        for copy in load(i):
            copy.start()
    row = lax.broadcasted_iota(jnp.int32, (ROWS, ROWS), 0)
    column = lax.broadcasted_iota(jnp.int32, (ROWS, ROWS), 1)
    own_gain = jnp.sum(jnp.where(row == column, gain[...].astype(F32), 0.0), axis=1, keepdims=True)
    row2 = lax.broadcasted_iota(jnp.int32, (ROWS, ROWS // 2), 0)
    column2 = lax.broadcasted_iota(jnp.int32, (ROWS, ROWS // 2), 1)
    own_scale = jnp.sum(jnp.where(row2 // 2 == column2, scales[...].astype(F32), 0.0), axis=1, keepdims=True)
    weight = (codes[...].astype(F32) * own_scale).astype(BF16)
    mine[...] = weight
    scaled = (weight.astype(F32) * own_gain).astype(BF16)
    start = 0
    for part in PARTS:
        gathered[part][z, x, y, core] = scaled[:, start : start + COLS[part]]
        start += COLS[part]

    barrier = pltpu.get_barrier_semaphore()
    partners = [sibling] + [beside(axis, step) for axis in range(3) for step in STEPS]
    for partner in partners:
        pl.semaphore_signal(barrier, inc=1, device_id=partner, device_id_type=MESH)
    columns_of_mask = mask[...].astype(F32).T
    for i in range(8):
        coef[pl.ds(128 * i, 128), :] = columns_of_mask[:, i : i + 1]
    pl.semaphore_wait(barrier, len(partners))

    ag_send_out(0)
    norms(0)
    norms(1)
    ag_wait(0)
    ag_send_out(1)
    chunk_out(0)
    norms(2)
    norms(3)
    partial_sums(0)
    pair_out(0)
    chunk_pass(0)
    partial_sums(1)
    pair_out(1)
    ag_wait(1)
    for chunk in (1, 2, 3):
        chunk_out(chunk)
    for part in PARTS:
        forward(part, 0, 0, False).start()
    pair_add(0)
    partial_sums(2)
    pair_out(2)
    pair_add(1)
    partial_sums(3)
    pair_out(3)
    pair_add(2)
    chunk_pass(1)
    pair_add(3)
    chunk_pass(2)
    chunk_pass(3)
    for i in range(4):
        rs_begin(i)
    for chunk in range(4):
        chunk_end(chunk)
    for slot in range(4):
        forward_wait(slot)
    project(0)
    rs_pass_z(0)
    rs_pass_z(1)
    rs_pass(0)
    rs_pass(1)
    project(1)
    rs_pass(2)
    rs_pass(3)
    project(2)
    project(3)
    project_end()
    rs_own_z()
    rs_send_out(0, 1)
    for part in (1, 2):
        rs_own(part)
        rs_send_out(part, 1)
    backward(0)
    backward(1)
    backward(2)
    for part in PARTS:
        rs_total(part, 1)
        rs_send_out(part, 2)
    backward(3)
    total = jnp.concatenate([rs_total(part, 2) for part in PARTS], axis=1)
    grad_weight[...] = total * own_gain
    sums_of_rows = jnp.sum(total * mine[...].astype(F32), axis=1, keepdims=True)
    grad_gain[...] = jnp.sum(jnp.where(row == column, sums_of_rows, 0.0), axis=0, keepdims=True)

    for part in PARTS:
        for stage in (0, 1):
            for slot in range(3):
                ag_copy(part, stage, slot, False).wait_send()
                rs_copy(part, stage + 1, slot).wait_send()
        forward(part, 0, 0, False).wait_send()
        for i in range(4):
            for slot in range(4):
                ag_chunk(part, i, slot, False).wait_send()
            for slot in (1, 2, 3):
                forward(part, i, slot, False).wait_send()
            pair_copy(part, i).wait_send()
    for slot in range(6):
        z_copy(slot).wait_send()
    for part in (1, 2):
        for i in range(4):
            for kind in range(3):
                block_copy(part, i, kind).wait_send()


def store(proj, tok, grad_weight, grad_gain, *refs):
    outs, sems = refs[:4], refs[4]
    copies = [
        pltpu.make_async_copy(src, dst, sems.at[i])
        for i, (src, dst) in enumerate(zip((proj, tok, grad_weight, grad_gain), outs))
    ]
    for copy in copies:
        copy.start()
    for copy in copies:
        copy.wait()


def shards(tokens, norm_gain, weight_codes, block_scales, upstream, loss_mask):
    anywhere = pl.BlockSpec(memory_space=pl.ANY)
    vmem = pl.BlockSpec(memory_space=pltpu.VMEM)
    blocks = [pltpu.VMEM((4, 4, 4, 2, ROWS, cols), BF16) for cols in COLS]
    pairs = [pltpu.VMEM((4, 4, 4, ROWS, cols), BF16) for cols in COLS]
    landing = [
        pltpu.VMEM((6, 2, 4, ROWS, COLS[0]), BF16),
        pltpu.VMEM((12, 4, ROWS, COLS[1]), BF16),
        pltpu.VMEM((12, 4, ROWS, COLS[2]), BF16),
        *[pltpu.VMEM((3, 4, ROWS, cols), BF16) for cols in COLS],
        *[pltpu.VMEM((3, ROWS, cols), BF16) for cols in COLS],
    ]
    dma = pltpu.SemaphoreType.DMA
    shapes = (((TOK, KV), BF16), ((TOK, D), BF16), ((ROWS, KV), F32), ((1, ROWS), F32))
    results = pl.pallas_call(
        kernel,
        out_shape=tuple(pltpu.VMEM(*shape) for shape in shapes),
        in_specs=[anywhere, anywhere, vmem, vmem, vmem, vmem],
        out_specs=(vmem, vmem, vmem, vmem),
        scratch_shapes=[
            pltpu.VMEM((TOK, KV), BF16),
            pltpu.VMEM((TOK, KV), BF16),
            pltpu.VMEM((TOK, KV), BF16),
            pltpu.VMEM((TOK, 1), F32),
            pltpu.VMEM((TOK, 1), F32),
            pltpu.VMEM((TOK, KV), F32),
            pltpu.VMEM((ROWS, KV), BF16),
            *blocks,
            *blocks,
            *pairs,
            *landing,
            dma((8,)),
            dma((66,)),
            dma((66,)),
            dma((39,)),
            dma((39,)),
            dma((12,)),
            dma((12,)),
            dma((54,)),
            dma((54,)),
        ],
        compiler_params=pltpu.CompilerParams(
            collective_id=0, has_side_effects=True, vmem_limit_bytes=48 * 1024 * 1024
        ),
        name="fused_key_projection",
    )(
        tokens,
        upstream,
        loss_mask.reshape(8, 128),
        weight_codes,
        block_scales.reshape(1, ROWS // 2),
        norm_gain.reshape(1, ROWS),
    )
    projected, grad_tokens, grad_weight, grad_gain = pl.pallas_call(
        store,
        out_shape=tuple(jax.ShapeDtypeStruct(*shape) for shape in shapes),
        in_specs=[vmem] * 4,
        out_specs=(anywhere,) * 4,
        scratch_shapes=[dma((4,))],
        compiler_params=pltpu.CompilerParams(vmem_limit_bytes=1024 * 1024),
        name="store_results",
    )(*[pltpu.with_memory_space_constraint(result, pltpu.VMEM) for result in results])
    return projected, grad_tokens, grad_weight, grad_gain.reshape(ROWS)


def solution(mesh):
    both = ("intra", "cross")
    return jax.shard_map(
        shards,
        mesh=mesh,
        in_specs=(P(both, None), P(both), P(both, None), P(both), P(both, None), P(both)),
        out_specs=(P(both, None), P(both, None), P(both, None), P(both)),
        check_vma=False,
    )
```

```python
import jax
import jax.numpy as jnp
from jax import lax
from jax.experimental import pallas as pl
from jax.experimental.pallas import tpu as pltpu
from jax.sharding import PartitionSpec as P

MESH = pl.DeviceIdType.MESH
F32 = jnp.float32
BF16 = jnp.bfloat16
D = 4096
KV = 1024
TOK = 1024
ROWS = 32
TILE = 256
COLS = (384, 384, 256)
ORDERS = ((0, 1, 2), (1, 2, 0), (2, 0, 1))
PARTS = range(3)
STEPS = (1, -1, 2)
CHUNKS = (0, 1, -1, 2)
PLANES = (0, -1, 1, 2)


def piece(part, stage, pos, at, half=None):
    order = ORDERS[part]
    index = [None, None, None, pos[3], slice(None), slice(None)]
    for axis in order[:stage]:
        index[axis] = pos[axis]
    index[order[stage]] = at
    free = order[stage + 1 :]
    for axis in free:
        index[axis] = slice(None)
    if half is not None:
        if free:
            index[min(free)] = slice(2 * half, 2 * half + 2)
        else:
            index[4] = slice(16 * half, 16 * half + 16)
    return tuple(index)


def kernel(
    tokens, upstream, mask, codes, scales, gain,
    proj, tok, grad_weight, grad_gain,
    up, masked, mi, inv, coef, acc, mine,
    w0, w1, w2, g0, g1, g2, c0, c1, c2,
    r00, r10, r20, r01, r11, r21, r02, r12, r22,
    load_sem, ag_send, ag_recv, fwd_send, fwd_recv, pair_send, pair_recv, rs_send, rs_recv,
):
    gathered = (w0, w1, w2)
    sums = (g0, g1, g2)
    pair = (c0, c1, c2)
    landing = ((r00, r01, r02), (r10, r11, r12), (r20, r21, r22))
    intra, cross = lax.axis_index("intra"), lax.axis_index("cross")
    z, x, y, core = intra // 4, intra % 4, cross // 2, cross % 2
    pos = (z, x, y, core)

    def device(at):
        return (at[0] * 4 + at[1], at[2] * 2 + at[3])

    def shifted(axis, step):
        return (pos[axis] + step + 4) % 4

    def beside(axis, step):
        return device(pos[:axis] + (shifted(axis, step),) + pos[axis + 1 :])

    sibling = device((z, x, y, 1 - core))
    blocks = [shifted(0, step) for step in (2, 1, 3, 0)]

    def remote(src, dst, send, recv, to):
        return pltpu.make_async_remote_copy(
            src_ref=src, dst_ref=dst, send_sem=send, recv_sem=recv, device_id=to, device_id_type=MESH
        )

    def ag_copy(part, stage, slot, arriving):
        axis = ORDERS[part][2 - stage]
        at = shifted(axis, -STEPS[slot]) if arriving else pos[axis]
        ref = gathered[part].at[piece(part, 2 - stage, pos, at)]
        number = part * 22 + stage * 3 + slot
        return remote(ref, ref, ag_send.at[number], ag_recv.at[number], beside(axis, STEPS[slot]))

    def ag_chunk(part, chunk, slot, arriving):
        far, near, last = ORDERS[part]
        side = (1, -1, 1, -1)[slot]
        hops = 1 if slot < 2 else 2
        came = hops if arriving else hops - 1
        index = [None, None, None, core, slice(None), slice(None)]
        index[far] = shifted(far, -side * came)
        index[near] = shifted(near, -CHUNKS[chunk])
        index[last] = slice(None) if slot < 2 else slice(2 * (slot - 2), 2 * (slot - 2) + 2)
        ref = gathered[part].at[tuple(index)]
        number = part * 22 + 6 + chunk * 4 + slot
        return remote(ref, ref, ag_send.at[number], ag_recv.at[number], beside(far, side))

    def forward(part, chunk, slot, arriving):
        far, near, _ = ORDERS[part]
        index = [slice(None), slice(None), slice(None), (1 - core) if arriving else core, slice(None), slice(None)]
        index[far] = shifted(far, PLANES[slot])
        if slot:
            index[near] = shifted(near, -CHUNKS[chunk])
        ref = gathered[part].at[tuple(index)]
        number = part * 13 + (slot and 3 * chunk + slot)
        return remote(ref, ref, fwd_send.at[number], fwd_recv.at[number], sibling)

    def ag_send_out(stage):
        for part in PARTS:
            for slot in range(3):
                ag_copy(part, stage, slot, False).start()

    def ag_wait(stage, slots=range(3)):
        for part in PARTS:
            for slot in slots:
                ag_copy(part, stage, slot, True).wait_recv()

    def chunk_out(chunk):
        for part in PARTS:
            ag_chunk(part, chunk, 0, False).start()
            ag_chunk(part, chunk, 1, False).start()

    def chunk_pass(chunk):
        for part in PARTS:
            for side in (0, 1):
                ag_chunk(part, chunk, side, True).wait_recv()
                ag_chunk(part, chunk, 2 + side, False).start()
                forward(part, chunk, 1 + side, False).start()

    def chunk_end(chunk):
        for part in PARTS:
            ag_chunk(part, chunk, 2, True).wait_recv()
            ag_chunk(part, chunk, 3, True).wait_recv()
            forward(part, chunk, 3, False).start()

    def forward_wait(slot):
        for part in PARTS:
            for chunk in range(4 if slot else 1):
                forward(part, chunk, slot, True).wait_recv()

    def pair_copy(part, i):
        at, k = blocks[i], part * 4 + i
        index = (at, slice(None), slice(None), 1 - core)
        return remote(sums[part].at[index], pair[part].at[at], pair_send.at[k], pair_recv.at[k], sibling)

    def pair_out(i):
        for part in PARTS:
            pair_copy(part, i).start()

    def pair_add(i):
        at = blocks[i]
        for part in PARTS:
            pair_copy(part, i).wait_recv()

            def add(xi, carry, part=part):
                own = sums[part][at, xi, :, core].astype(F32)
                sums[part][at, xi, :, core] = (own + pair[part][at, xi].astype(F32)).astype(BF16)
                return carry

            lax.fori_loop(0, 4, add, 0)

    def rs_remote(part, stage, slot, index, axis, step):
        number = part * 18 + (0, 12, 15)[stage] + slot
        return remote(
            sums[part].at[index], landing[part][stage].at[slot],
            rs_send.at[number], rs_recv.at[number], beside(axis, step),
        )

    def z_copy(slot):
        step, half, side = ((2, 0, 1), (2, 1, -1), (1, 0, 1), (1, 1, 1), (-1, 0, -1), (-1, 1, -1))[slot]
        return rs_remote(0, 0, slot, piece(0, 0, pos, shifted(0, step), half), 0, side)

    def block_index(part, i, at):
        index = [blocks[i], slice(None), slice(None), core, slice(None), slice(None)]
        index[ORDERS[part][0]] = at
        return tuple(index)

    def block_copy(part, i, kind):
        axis = ORDERS[part][0]
        side = ((1 if i < 2 else -1), 1, -1)[kind]
        step = (2, 1, -1)[kind]
        return rs_remote(part, 0, kind * 4 + i, block_index(part, i, shifted(axis, step)), axis, side)

    def rs_across(i):
        if i == 0:
            z_copy(0).start()
            z_copy(1).start()
        for part in (1, 2):
            block_copy(part, i, 0).start()

    def rs_direct(i):
        if i in (1, 2):
            z_copy(2 + i).start()
        for part in (1, 2):
            block_copy(part, i, 2 if i < 2 else 1).start()

    def rs_pass_z(slot):
        out = (2, 5)[slot]
        z_copy(slot).wait_recv()
        index = piece(0, 0, pos, shifted(0, (1, -1)[slot]), slot)
        sums[0][index] = (sums[0][index].astype(F32) + landing[0][0][slot].astype(F32)).astype(BF16)
        z_copy(out).start()

    def rs_pass(i):
        for part in (1, 2):
            block_copy(part, i, 0).wait_recv()
            step, kind = (1, 1) if i < 2 else (-1, 2)
            index = block_index(part, i, shifted(ORDERS[part][0], step))
            sums[part][index] = (sums[part][index].astype(F32) + landing[part][0][i].astype(F32)).astype(BF16)
            block_copy(part, i, kind).start()

    def rs_own_z():
        for slot in (2, 3, 4, 5):
            z_copy(slot).wait_recv()
        for half in (0, 1):
            index = piece(0, 0, pos, z, half)
            sums[0][index] = (
                sums[0][index].astype(F32)
                + landing[0][0][2 + half].astype(F32)
                + landing[0][0][4 + half].astype(F32)
            ).astype(BF16)

    def rs_own(part):
        for i in range(4):
            block_copy(part, i, 1).wait_recv()
            block_copy(part, i, 2).wait_recv()
            index = block_index(part, i, pos[ORDERS[part][0]])
            sums[part][index] = (
                sums[part][index].astype(F32)
                + landing[part][0][4 + i].astype(F32)
                + landing[part][0][8 + i].astype(F32)
            ).astype(BF16)

    def rs_copy(part, stage, slot):
        axis = ORDERS[part][stage]
        index = piece(part, stage, pos, shifted(axis, STEPS[slot]))
        return rs_remote(part, stage, slot, index, axis, STEPS[slot])

    def rs_send_out(part, stage):
        for slot in (2, 0, 1):
            rs_copy(part, stage, slot).start()

    def rs_total(part, stage):
        index = piece(part, stage, pos, pos[ORDERS[part][stage]])
        total = sums[part][index].astype(F32)
        for slot in range(3):
            rs_copy(part, stage, slot).wait_recv()
            total = total + landing[part][stage][slot].astype(F32)
        if stage == 1:
            sums[part][index] = total.astype(BF16)
        return total

    def load(i):
        rows = pl.ds(i * TILE, TILE)
        return (
            pltpu.make_async_copy(tokens.at[rows], tok.at[rows], load_sem.at[i]),
            pltpu.make_async_copy(upstream.at[rows], up.at[rows], load_sem.at[4 + i]),
        )

    def norms(i):
        for copy in load(i):
            copy.wait()

        def some(j, carry):
            rows = pl.ds(pl.multiple_of(i * TILE + j * 64, 64), 64)
            values = tok[rows, :].astype(F32)
            inverse = lax.rsqrt(jnp.sum(values * values, axis=1, keepdims=True) * (1.0 / D) + 1e-05)
            inv[rows, :] = inverse
            kept = up[rows, :].astype(F32) * coef[rows, :]
            masked[rows, :] = kept.astype(BF16)
            mi[rows, :] = (kept * inverse).astype(BF16)
            return carry

        lax.fori_loop(0, TILE // 64, some, 0)

    def partial_sums(i):
        zi = blocks[i]
        columns = pl.ds(pl.multiple_of(zi * 1024, 1024), 1024)
        part_sum = lax.dot_general(
            tok[:, columns], mi[...], (((0,), (0,)), ((), ())), preferred_element_type=F32
        ).astype(BF16)
        start = 0
        for part in PARTS:
            cols = part_sum[:, start : start + COLS[part]]
            sums[part][zi] = cols.reshape(4, 4, 2, ROWS, COLS[part])
            start += COLS[part]

    def weight_block(zi):
        return jnp.concatenate(
            [gathered[part][zi].reshape(1024, COLS[part]) for part in PARTS], axis=1
        )

    def project(part, number, at):
        start = sum(COLS[:part])
        cols = slice(start, start + COLS[part])
        if part == 0:
            left, right = tok[:, pl.ds(pl.multiple_of(at * 1024, 1024), 1024)], gathered[0][at].reshape(1024, COLS[0])
        elif part == 1:
            left = [tok[:, pl.ds(pl.multiple_of(zi * 1024 + at * 256, 256), 256)] for zi in range(4)]
            right = [gathered[1][zi, at].reshape(256, COLS[1]) for zi in range(4)]
            left, right = jnp.concatenate(left, axis=1), jnp.concatenate(right, axis=0)
        else:
            left, right = tok[...], gathered[2][...].reshape(D, COLS[2])
        value = jnp.dot(left, right, preferred_element_type=F32)
        if number == 0:
            acc[:, cols] = value
        else:
            acc[:, cols] += value

    def project_planes(slot):
        for part in (0, 1):
            project(part, slot, shifted(ORDERS[part][0], PLANES[slot]))

    def project_end():
        def some(j):
            rows = pl.ds(j * 64, 64)
            inverse = inv[rows, :]
            value = acc[rows, :] * inverse
            proj[rows, :] = value.astype(BF16)
            mean = jnp.sum(value * masked[rows, :].astype(F32), axis=1, keepdims=True) * (1.0 / D)
            coef[rows, :] = mean * inverse

        for j in range(TOK // 64):
            some(j)

    def backward(zi):
        columns = pl.ds(zi * 1024, 1024)
        value = lax.dot_general(
            masked[...], weight_block(zi), (((1,), (1,)), ((), ())), preferred_element_type=F32
        )
        value = inv[...] * (value - tok[:, columns].astype(F32) * coef[...])
        tok[:, columns] = value.astype(BF16)

    barrier = pltpu.get_barrier_semaphore()
    partners = [sibling] + [beside(axis, step) for axis in range(3) for step in STEPS]
    for partner in partners:
        pl.semaphore_signal(barrier, inc=1, device_id=partner, device_id_type=MESH)
    for i in range(4):
        for copy in load(i):
            copy.start()
    row = lax.broadcasted_iota(jnp.int32, (ROWS, ROWS), 0)
    column = lax.broadcasted_iota(jnp.int32, (ROWS, ROWS), 1)
    own_gain = jnp.sum(jnp.where(row == column, gain[...].astype(F32), 0.0), axis=1, keepdims=True)
    row2 = lax.broadcasted_iota(jnp.int32, (ROWS, ROWS // 2), 0)
    column2 = lax.broadcasted_iota(jnp.int32, (ROWS, ROWS // 2), 1)
    own_scale = jnp.sum(jnp.where(row2 // 2 == column2, scales[...].astype(F32), 0.0), axis=1, keepdims=True)
    weight = (codes[...].astype(F32) * own_scale).astype(BF16)
    mine[...] = weight
    scaled = (weight.astype(F32) * own_gain).astype(BF16)
    start = 0
    for part in PARTS:
        gathered[part][z, x, y, core] = scaled[:, start : start + COLS[part]]
        start += COLS[part]

    columns_of_mask = mask[...].astype(F32).T
    for i in range(8):
        coef[pl.ds(128 * i, 128), :] = columns_of_mask[:, i : i + 1]
    pl.semaphore_wait(barrier, len(partners))

    ag_send_out(0)
    norms(0)
    norms(1)
    ag_wait(0)
    ag_send_out(1)
    chunk_out(0)
    norms(2)
    norms(3)
    partial_sums(0)
    pair_out(0)
    partial_sums(1)
    pair_out(1)
    ag_wait(1)
    for chunk in (1, 2, 3):
        chunk_out(chunk)
    for part in PARTS:
        forward(part, 0, 0, False).start()
    pair_add(0)
    partial_sums(2)
    pair_out(2)
    chunk_pass(0)
    pair_add(1)
    rs_across(0)
    rs_across(1)
    partial_sums(3)
    pair_out(3)
    pair_add(2)
    rs_across(2)
    chunk_pass(1)
    pair_add(3)
    rs_across(3)
    chunk_pass(2)
    chunk_pass(3)
    for i in range(4):
        rs_direct(i)
    forward_wait(0)
    project_planes(0)
    forward_wait(1)
    project_planes(1)
    rs_pass_z(0)
    rs_pass_z(1)
    for i in range(4):
        rs_pass(i)
    forward_wait(2)
    project_planes(2)
    for chunk in range(4):
        chunk_end(chunk)
    forward_wait(3)
    project_planes(3)
    project(2, 0, 0)
    project_end()
    backward(0)
    rs_own_z()
    rs_send_out(0, 1)
    for part in (1, 2):
        rs_own(part)
        rs_send_out(part, 1)
    backward(1)
    backward(2)
    for part in PARTS:
        rs_total(part, 1)
        rs_send_out(part, 2)
    backward(3)
    total = jnp.concatenate([rs_total(part, 2) for part in PARTS], axis=1)
    grad_weight[...] = total * own_gain
    sums_of_rows = jnp.sum(total * mine[...].astype(F32), axis=1, keepdims=True)
    grad_gain[...] = jnp.sum(jnp.where(row == column, sums_of_rows, 0.0), axis=0, keepdims=True)

    for part in PARTS:
        for stage in (0, 1):
            for slot in range(3):
                ag_copy(part, stage, slot, False).wait_send()
                rs_copy(part, stage + 1, slot).wait_send()
        forward(part, 0, 0, False).wait_send()
        for i in range(4):
            for slot in range(4):
                ag_chunk(part, i, slot, False).wait_send()
            for slot in (1, 2, 3):
                forward(part, i, slot, False).wait_send()
            pair_copy(part, i).wait_send()
    for slot in range(6):
        z_copy(slot).wait_send()
    for part in (1, 2):
        for i in range(4):
            for kind in range(3):
                block_copy(part, i, kind).wait_send()


def store(proj, tok, grad_weight, grad_gain, *refs):
    outs, sems = refs[:4], refs[4]
    copies = [
        pltpu.make_async_copy(src, dst, sems.at[i])
        for i, (src, dst) in enumerate(zip((proj, tok, grad_weight, grad_gain), outs))
    ]
    for copy in copies:
        copy.start()
    for copy in copies:
        copy.wait()


def shards(tokens, norm_gain, weight_codes, block_scales, upstream, loss_mask):
    anywhere = pl.BlockSpec(memory_space=pl.ANY)
    vmem = pl.BlockSpec(memory_space=pltpu.VMEM)
    blocks = [pltpu.VMEM((4, 4, 4, 2, ROWS, cols), BF16) for cols in COLS]
    pairs = [pltpu.VMEM((4, 4, 4, ROWS, cols), BF16) for cols in COLS]
    landing = [
        pltpu.VMEM((6, 2, 4, ROWS, COLS[0]), BF16),
        pltpu.VMEM((12, 4, ROWS, COLS[1]), BF16),
        pltpu.VMEM((12, 4, ROWS, COLS[2]), BF16),
        *[pltpu.VMEM((3, 4, ROWS, cols), BF16) for cols in COLS],
        *[pltpu.VMEM((3, ROWS, cols), BF16) for cols in COLS],
    ]
    dma = pltpu.SemaphoreType.DMA
    shapes = (((TOK, KV), BF16), ((TOK, D), BF16), ((ROWS, KV), F32), ((1, ROWS), F32))
    results = pl.pallas_call(
        kernel,
        out_shape=tuple(pltpu.VMEM(*shape) for shape in shapes),
        in_specs=[anywhere, anywhere, vmem, vmem, vmem, vmem],
        out_specs=(vmem, vmem, vmem, vmem),
        scratch_shapes=[
            pltpu.VMEM((TOK, KV), BF16),
            pltpu.VMEM((TOK, KV), BF16),
            pltpu.VMEM((TOK, KV), BF16),
            pltpu.VMEM((TOK, 1), F32),
            pltpu.VMEM((TOK, 1), F32),
            pltpu.VMEM((TOK, KV), F32),
            pltpu.VMEM((ROWS, KV), BF16),
            *blocks,
            *blocks,
            *pairs,
            *landing,
            dma((8,)),
            dma((66,)),
            dma((66,)),
            dma((39,)),
            dma((39,)),
            dma((12,)),
            dma((12,)),
            dma((54,)),
            dma((54,)),
        ],
        compiler_params=pltpu.CompilerParams(
            collective_id=0, has_side_effects=True, vmem_limit_bytes=48 * 1024 * 1024
        ),
        name="fused_key_projection",
    )(
        tokens,
        upstream,
        loss_mask.reshape(8, 128),
        weight_codes,
        block_scales.reshape(1, ROWS // 2),
        norm_gain.reshape(1, ROWS),
    )
    projected, grad_tokens, grad_weight, grad_gain = pl.pallas_call(
        store,
        out_shape=tuple(jax.ShapeDtypeStruct(*shape) for shape in shapes),
        in_specs=[vmem] * 4,
        out_specs=(anywhere,) * 4,
        scratch_shapes=[dma((4,))],
        compiler_params=pltpu.CompilerParams(vmem_limit_bytes=1024 * 1024),
        name="store_results",
    )(*[pltpu.with_memory_space_constraint(result, pltpu.VMEM) for result in results])
    return projected, grad_tokens, grad_weight, grad_gain.reshape(ROWS)


def solution(mesh):
    both = ("intra", "cross")
    return jax.shard_map(
        shards,
        mesh=mesh,
        in_specs=(P(both, None), P(both), P(both, None), P(both), P(both, None), P(both)),
        out_specs=(P(both, None), P(both, None), P(both, None), P(both)),
        check_vma=False,
    )
```

```python
import jax
import jax.numpy as jnp
from jax import lax
from jax.experimental import pallas as pl
from jax.experimental.pallas import tpu as pltpu
from jax.sharding import PartitionSpec as P

MESH = pl.DeviceIdType.MESH
F32 = jnp.float32
BF16 = jnp.bfloat16
D = 4096
KV = 1024
TOK = 1024
ROWS = 32
TILE = 256
COLS = (384, 384, 256)
ORDERS = ((0, 1, 2), (1, 2, 0), (2, 0, 1))
PARTS = range(3)
STEPS = (1, -1, 2)
CHUNKS = (0, 1, -1, 2)
PLANES = (0, -1, 1, 2)


def piece(part, stage, pos, at, half=None):
    order = ORDERS[part]
    index = [None, None, None, pos[3], slice(None), slice(None)]
    for axis in order[:stage]:
        index[axis] = pos[axis]
    index[order[stage]] = at
    free = order[stage + 1 :]
    for axis in free:
        index[axis] = slice(None)
    if half is not None:
        if free:
            index[min(free)] = slice(2 * half, 2 * half + 2)
        else:
            index[4] = slice(16 * half, 16 * half + 16)
    return tuple(index)


def kernel(
    tokens, upstream, mask, codes, scales, gain,
    proj, tok, grad_weight, grad_gain,
    up, masked, mi, inv, coef, acc, mine,
    w0, w1, w2, g0, g1, g2, c0, c1, c2,
    r00, r10, r20, r01, r11, r21, r02, r12, r22,
    load_sem, ag_send, ag_recv, fwd_send, fwd_recv, pair_send, pair_recv, rs_send, rs_recv,
):
    gathered = (w0, w1, w2)
    sums = (g0, g1, g2)
    pair = (c0, c1, c2)
    landing = ((r00, r01, r02), (r10, r11, r12), (r20, r21, r22))
    intra, cross = lax.axis_index("intra"), lax.axis_index("cross")
    z, x, y, core = intra // 4, intra % 4, cross // 2, cross % 2
    pos = (z, x, y, core)

    def device(at):
        return (at[0] * 4 + at[1], at[2] * 2 + at[3])

    def shifted(axis, step):
        return (pos[axis] + step + 4) % 4

    def beside(axis, step):
        return device(pos[:axis] + (shifted(axis, step),) + pos[axis + 1 :])

    sibling = device((z, x, y, 1 - core))
    blocks = [shifted(0, step) for step in (2, 1, 3, 0)]

    def remote(src, dst, send, recv, to):
        return pltpu.make_async_remote_copy(
            src_ref=src, dst_ref=dst, send_sem=send, recv_sem=recv, device_id=to, device_id_type=MESH
        )

    def ag_copy(part, stage, slot, arriving):
        axis = ORDERS[part][2 - stage]
        at = shifted(axis, -STEPS[slot]) if arriving else pos[axis]
        ref = gathered[part].at[piece(part, 2 - stage, pos, at)]
        number = part * 22 + stage * 3 + slot
        return remote(ref, ref, ag_send.at[number], ag_recv.at[number], beside(axis, STEPS[slot]))

    def ag_chunk(part, chunk, slot, arriving):
        far, near, last = ORDERS[part]
        side = (1, -1, 1, -1)[slot]
        hops = 1 if slot < 2 else 2
        came = hops if arriving else hops - 1
        index = [None, None, None, core, slice(None), slice(None)]
        index[far] = shifted(far, -side * came)
        index[near] = shifted(near, -CHUNKS[chunk])
        index[last] = slice(None) if slot < 2 else slice(2 * (slot - 2), 2 * (slot - 2) + 2)
        ref = gathered[part].at[tuple(index)]
        number = part * 22 + 6 + chunk * 4 + slot
        return remote(ref, ref, ag_send.at[number], ag_recv.at[number], beside(far, side))

    def forward(part, chunk, slot, arriving):
        far, near, _ = ORDERS[part]
        index = [slice(None), slice(None), slice(None), (1 - core) if arriving else core, slice(None), slice(None)]
        index[far] = shifted(far, PLANES[slot])
        if slot:
            index[near] = shifted(near, -CHUNKS[chunk])
        ref = gathered[part].at[tuple(index)]
        number = part * 13 + (slot and 3 * chunk + slot)
        return remote(ref, ref, fwd_send.at[number], fwd_recv.at[number], sibling)

    def ag_send_out(stage):
        for part in PARTS:
            for slot in range(3):
                ag_copy(part, stage, slot, False).start()

    def ag_wait(stage, slots=range(3)):
        for part in PARTS:
            for slot in slots:
                ag_copy(part, stage, slot, True).wait_recv()

    def chunk_out(chunk):
        for part in PARTS:
            ag_chunk(part, chunk, 0, False).start()
            ag_chunk(part, chunk, 1, False).start()

    def chunk_pass(chunk):
        for part in PARTS:
            for side in (0, 1):
                ag_chunk(part, chunk, side, True).wait_recv()
                ag_chunk(part, chunk, 2 + side, False).start()
                forward(part, chunk, 1 + side, False).start()

    def chunk_end(chunk):
        for part in PARTS:
            ag_chunk(part, chunk, 2, True).wait_recv()
            ag_chunk(part, chunk, 3, True).wait_recv()
            forward(part, chunk, 3, False).start()

    def forward_wait(slot):
        for part in PARTS:
            for chunk in range(4 if slot else 1):
                forward(part, chunk, slot, True).wait_recv()

    def pair_copy(part, i):
        at, k = blocks[i], part * 4 + i
        index = (at, slice(None), slice(None), 1 - core)
        return remote(sums[part].at[index], pair[part].at[at], pair_send.at[k], pair_recv.at[k], sibling)

    def pair_out(i):
        for part in PARTS:
            pair_copy(part, i).start()

    def pair_add(i):
        at = blocks[i]
        for part in PARTS:
            pair_copy(part, i).wait_recv()

            def add(xi, carry, part=part):
                own = sums[part][at, xi, :, core].astype(F32)
                sums[part][at, xi, :, core] = (own + pair[part][at, xi].astype(F32)).astype(BF16)
                return carry

            lax.fori_loop(0, 4, add, 0)

    def rs_remote(part, stage, slot, index, axis, step):
        number = part * 18 + (0, 12, 15)[stage] + slot
        return remote(
            sums[part].at[index], landing[part][stage].at[slot],
            rs_send.at[number], rs_recv.at[number], beside(axis, step),
        )

    def z_copy(slot):
        step, half, side = ((2, 0, 1), (2, 1, -1), (1, 0, 1), (1, 1, 1), (-1, 0, -1), (-1, 1, -1))[slot]
        return rs_remote(0, 0, slot, piece(0, 0, pos, shifted(0, step), half), 0, side)

    def block_index(part, i, at):
        index = [blocks[i], slice(None), slice(None), core, slice(None), slice(None)]
        index[ORDERS[part][0]] = at
        return tuple(index)

    def block_copy(part, i, kind):
        axis = ORDERS[part][0]
        side = ((1 if i < 2 else -1), 1, -1)[kind]
        step = (2, 1, -1)[kind]
        return rs_remote(part, 0, kind * 4 + i, block_index(part, i, shifted(axis, step)), axis, side)

    def rs_across(i):
        if i == 0:
            z_copy(0).start()
            z_copy(1).start()
        for part in (1, 2):
            block_copy(part, i, 0).start()

    def rs_direct(i):
        if i in (1, 2):
            z_copy(2 + i).start()
        for part in (1, 2):
            block_copy(part, i, 2 if i < 2 else 1).start()

    def rs_pass_z(slot):
        out = (2, 5)[slot]
        z_copy(slot).wait_recv()
        index = piece(0, 0, pos, shifted(0, (1, -1)[slot]), slot)
        sums[0][index] = (sums[0][index].astype(F32) + landing[0][0][slot].astype(F32)).astype(BF16)
        z_copy(out).start()

    def rs_pass(i):
        for part in (1, 2):
            block_copy(part, i, 0).wait_recv()
            step, kind = (1, 1) if i < 2 else (-1, 2)
            index = block_index(part, i, shifted(ORDERS[part][0], step))
            sums[part][index] = (sums[part][index].astype(F32) + landing[part][0][i].astype(F32)).astype(BF16)
            block_copy(part, i, kind).start()

    def rs_own_z():
        for slot in (2, 3, 4, 5):
            z_copy(slot).wait_recv()
        for half in (0, 1):
            index = piece(0, 0, pos, z, half)
            sums[0][index] = (
                sums[0][index].astype(F32)
                + landing[0][0][2 + half].astype(F32)
                + landing[0][0][4 + half].astype(F32)
            ).astype(BF16)

    def rs_own(part):
        for i in range(4):
            block_copy(part, i, 1).wait_recv()
            block_copy(part, i, 2).wait_recv()
            index = block_index(part, i, pos[ORDERS[part][0]])
            sums[part][index] = (
                sums[part][index].astype(F32)
                + landing[part][0][4 + i].astype(F32)
                + landing[part][0][8 + i].astype(F32)
            ).astype(BF16)

    def rs_copy(part, stage, slot):
        axis = ORDERS[part][stage]
        index = piece(part, stage, pos, shifted(axis, STEPS[slot]))
        return rs_remote(part, stage, slot, index, axis, STEPS[slot])

    def rs_send_out(part, stage):
        for slot in (2, 0, 1):
            rs_copy(part, stage, slot).start()

    def rs_total(part, stage):
        index = piece(part, stage, pos, pos[ORDERS[part][stage]])
        total = sums[part][index].astype(F32)
        for slot in range(3):
            rs_copy(part, stage, slot).wait_recv()
            total = total + landing[part][stage][slot].astype(F32)
        if stage == 1:
            sums[part][index] = total.astype(BF16)
        return total

    def load(i):
        rows = pl.ds(i * TILE, TILE)
        return (
            pltpu.make_async_copy(tokens.at[rows], tok.at[rows], load_sem.at[i]),
            pltpu.make_async_copy(upstream.at[rows], up.at[rows], load_sem.at[4 + i]),
        )

    def norms(i):
        for copy in load(i):
            copy.wait()

        def some(j, carry):
            rows = pl.ds(pl.multiple_of(i * TILE + j * 64, 64), 64)
            values = tok[rows, :].astype(F32)
            inverse = lax.rsqrt(jnp.sum(values * values, axis=1, keepdims=True) * (1.0 / D) + 1e-05)
            inv[rows, :] = inverse
            kept = up[rows, :].astype(F32) * coef[rows, :]
            masked[rows, :] = kept.astype(BF16)
            mi[rows, :] = (kept * inverse).astype(BF16)
            return carry

        lax.fori_loop(0, TILE // 64, some, 0)

    def partial_sums(i):
        zi = blocks[i]
        columns = pl.ds(pl.multiple_of(zi * 1024, 1024), 1024)
        part_sum = lax.dot_general(
            tok[:, columns], mi[...], (((0,), (0,)), ((), ())), preferred_element_type=F32
        ).astype(BF16)
        start = 0
        for part in PARTS:
            cols = part_sum[:, start : start + COLS[part]]
            sums[part][zi] = cols.reshape(4, 4, 2, ROWS, COLS[part])
            start += COLS[part]

    def weight_block(zi):
        return jnp.concatenate(
            [gathered[part][zi].reshape(1024, COLS[part]) for part in PARTS], axis=1
        )

    def project(part, number, at):
        start = sum(COLS[:part])
        cols = slice(start, start + COLS[part])
        if part == 0:
            left, right = tok[:, pl.ds(pl.multiple_of(at * 1024, 1024), 1024)], gathered[0][at].reshape(1024, COLS[0])
        elif part == 1:
            left = [tok[:, pl.ds(pl.multiple_of(zi * 1024 + at * 256, 256), 256)] for zi in range(4)]
            right = [gathered[1][zi, at].reshape(256, COLS[1]) for zi in range(4)]
            left, right = jnp.concatenate(left, axis=1), jnp.concatenate(right, axis=0)
        else:
            left, right = tok[...], gathered[2][...].reshape(D, COLS[2])
        value = jnp.dot(left, right, preferred_element_type=F32)
        if number == 0:
            acc[:, cols] = value
        else:
            acc[:, cols] += value

    def project_planes(slot):
        for part in (0, 1):
            project(part, slot, shifted(ORDERS[part][0], PLANES[slot]))

    def project_end():
        def some(j):
            rows = pl.ds(j * 64, 64)
            inverse = inv[rows, :]
            value = acc[rows, :] * inverse
            proj[rows, :] = value.astype(BF16)
            mean = jnp.sum(value * masked[rows, :].astype(F32), axis=1, keepdims=True) * (1.0 / D)
            coef[rows, :] = mean * inverse

        for j in range(TOK // 64):
            some(j)

    def backward(zi):
        columns = pl.ds(zi * 1024, 1024)
        value = lax.dot_general(
            masked[...], weight_block(zi), (((1,), (1,)), ((), ())), preferred_element_type=F32
        )
        value = inv[...] * (value - tok[:, columns].astype(F32) * coef[...])
        tok[:, columns] = value.astype(BF16)

    barrier = pltpu.get_barrier_semaphore()
    partners = [sibling] + [beside(axis, step) for axis in range(3) for step in STEPS]
    for partner in partners:
        pl.semaphore_signal(barrier, inc=1, device_id=partner, device_id_type=MESH)
    for i in range(4):
        for copy in load(i):
            copy.start()
    row = lax.broadcasted_iota(jnp.int32, (ROWS, ROWS), 0)
    column = lax.broadcasted_iota(jnp.int32, (ROWS, ROWS), 1)
    own_gain = jnp.sum(jnp.where(row == column, gain[...].astype(F32), 0.0), axis=1, keepdims=True)
    row2 = lax.broadcasted_iota(jnp.int32, (ROWS, ROWS // 2), 0)
    column2 = lax.broadcasted_iota(jnp.int32, (ROWS, ROWS // 2), 1)
    own_scale = jnp.sum(jnp.where(row2 // 2 == column2, scales[...].astype(F32), 0.0), axis=1, keepdims=True)
    weight = (codes[...].astype(F32) * own_scale).astype(BF16)
    mine[...] = weight
    scaled = (weight.astype(F32) * own_gain).astype(BF16)
    start = 0
    for part in PARTS:
        gathered[part][z, x, y, core] = scaled[:, start : start + COLS[part]]
        start += COLS[part]

    columns_of_mask = mask[...].astype(F32).T
    for i in range(8):
        coef[pl.ds(128 * i, 128), :] = columns_of_mask[:, i : i + 1]
    pl.semaphore_wait(barrier, len(partners))

    ag_send_out(0)
    norms(0)
    norms(1)
    ag_wait(0)
    ag_send_out(1)
    chunk_out(0)
    norms(2)
    norms(3)
    partial_sums(0)
    pair_out(0)
    partial_sums(1)
    pair_out(1)
    ag_wait(1)
    for chunk in (1, 2, 3):
        chunk_out(chunk)
    for part in PARTS:
        forward(part, 0, 0, False).start()
    pair_add(0)
    partial_sums(2)
    pair_out(2)
    chunk_pass(0)
    pair_add(1)
    rs_across(0)
    rs_across(1)
    partial_sums(3)
    pair_out(3)
    pair_add(2)
    rs_across(2)
    chunk_pass(1)
    pair_add(3)
    rs_across(3)
    chunk_pass(2)
    chunk_pass(3)
    forward_wait(0)
    project_planes(0)
    forward_wait(1)
    project_planes(1)
    rs_pass_z(0)
    rs_pass_z(1)
    for i in range(4):
        rs_pass(i)
    for i in range(4):
        rs_direct(i)
    for chunk in range(4):
        chunk_end(chunk)
    forward_wait(2)
    project_planes(2)
    forward_wait(3)
    project_planes(3)
    project(2, 0, 0)
    project_end()
    backward(0)
    rs_own_z()
    rs_send_out(0, 1)
    for part in (1, 2):
        rs_own(part)
        rs_send_out(part, 1)
    backward(1)
    backward(2)
    for part in PARTS:
        rs_total(part, 1)
        rs_send_out(part, 2)
    backward(3)
    total = jnp.concatenate([rs_total(part, 2) for part in PARTS], axis=1)
    grad_weight[...] = total * own_gain
    sums_of_rows = jnp.sum(total * mine[...].astype(F32), axis=1, keepdims=True)
    grad_gain[...] = jnp.sum(jnp.where(row == column, sums_of_rows, 0.0), axis=0, keepdims=True)

    for part in PARTS:
        for stage in (0, 1):
            for slot in range(3):
                ag_copy(part, stage, slot, False).wait_send()
                rs_copy(part, stage + 1, slot).wait_send()
        forward(part, 0, 0, False).wait_send()
        for i in range(4):
            for slot in range(4):
                ag_chunk(part, i, slot, False).wait_send()
            for slot in (1, 2, 3):
                forward(part, i, slot, False).wait_send()
            pair_copy(part, i).wait_send()
    for slot in range(6):
        z_copy(slot).wait_send()
    for part in (1, 2):
        for i in range(4):
            for kind in range(3):
                block_copy(part, i, kind).wait_send()


def store(proj, tok, grad_weight, grad_gain, *refs):
    outs, sems = refs[:4], refs[4]
    copies = [
        pltpu.make_async_copy(src, dst, sems.at[i])
        for i, (src, dst) in enumerate(zip((proj, tok, grad_weight, grad_gain), outs))
    ]
    for copy in copies:
        copy.start()
    for copy in copies:
        copy.wait()


def shards(tokens, norm_gain, weight_codes, block_scales, upstream, loss_mask):
    anywhere = pl.BlockSpec(memory_space=pl.ANY)
    vmem = pl.BlockSpec(memory_space=pltpu.VMEM)
    blocks = [pltpu.VMEM((4, 4, 4, 2, ROWS, cols), BF16) for cols in COLS]
    pairs = [pltpu.VMEM((4, 4, 4, ROWS, cols), BF16) for cols in COLS]
    landing = [
        pltpu.VMEM((6, 2, 4, ROWS, COLS[0]), BF16),
        pltpu.VMEM((12, 4, ROWS, COLS[1]), BF16),
        pltpu.VMEM((12, 4, ROWS, COLS[2]), BF16),
        *[pltpu.VMEM((3, 4, ROWS, cols), BF16) for cols in COLS],
        *[pltpu.VMEM((3, ROWS, cols), BF16) for cols in COLS],
    ]
    dma = pltpu.SemaphoreType.DMA
    shapes = (((TOK, KV), BF16), ((TOK, D), BF16), ((ROWS, KV), F32), ((1, ROWS), F32))
    results = pl.pallas_call(
        kernel,
        out_shape=tuple(pltpu.VMEM(*shape) for shape in shapes),
        in_specs=[anywhere, anywhere, vmem, vmem, vmem, vmem],
        out_specs=(vmem, vmem, vmem, vmem),
        scratch_shapes=[
            pltpu.VMEM((TOK, KV), BF16),
            pltpu.VMEM((TOK, KV), BF16),
            pltpu.VMEM((TOK, KV), BF16),
            pltpu.VMEM((TOK, 1), F32),
            pltpu.VMEM((TOK, 1), F32),
            pltpu.VMEM((TOK, KV), F32),
            pltpu.VMEM((ROWS, KV), BF16),
            *blocks,
            *blocks,
            *pairs,
            *landing,
            dma((8,)),
            dma((66,)),
            dma((66,)),
            dma((39,)),
            dma((39,)),
            dma((12,)),
            dma((12,)),
            dma((54,)),
            dma((54,)),
        ],
        compiler_params=pltpu.CompilerParams(
            collective_id=0, has_side_effects=True, vmem_limit_bytes=48 * 1024 * 1024
        ),
        name="fused_key_projection",
    )(
        tokens,
        upstream,
        loss_mask.reshape(8, 128),
        weight_codes,
        block_scales.reshape(1, ROWS // 2),
        norm_gain.reshape(1, ROWS),
    )
    projected, grad_tokens, grad_weight, grad_gain = pl.pallas_call(
        store,
        out_shape=tuple(jax.ShapeDtypeStruct(*shape) for shape in shapes),
        in_specs=[vmem] * 4,
        out_specs=(anywhere,) * 4,
        scratch_shapes=[dma((4,))],
        compiler_params=pltpu.CompilerParams(vmem_limit_bytes=1024 * 1024),
        name="store_results",
    )(*[pltpu.with_memory_space_constraint(result, pltpu.VMEM) for result in results])
    return projected, grad_tokens, grad_weight, grad_gain.reshape(ROWS)


def solution(mesh):
    both = ("intra", "cross")
    return jax.shard_map(
        shards,
        mesh=mesh,
        in_specs=(P(both, None), P(both), P(both, None), P(both), P(both, None), P(both)),
        out_specs=(P(both, None), P(both, None), P(both, None), P(both)),
        check_vma=False,
    )
```
